32 devices in a mesh: run: 2 (over y), particle: 4 (over z), space: 4 (over x, core).
Axes of the slice: x: 2, y: 2, z: 4, core: 2. Of those that a mesh axis runs over, the one named last changes fastest.
Arguments:
- state: float32 [8, 8, 64, 1024], P(('run', 'particle'), None, 'space'), parts along dimension 0, may hold values from -6 to 6
- ancestors: int32 [8], P('run'), parts along dimension 0, may hold values from 0 to 3, as said below
- noise: bfloat16 [8, 2, 64, 1024], P(('run', 'particle'), None, 'space'), parts along dimension 0, may hold values from -6 to 6
Outputs:
- analysis: float32 [8, 8, 64, 1024], P(('run', 'particle'), None, 'space'), parts along dimension 0
The draws below stay inside these ranges and needn't reach their ends.
There are 2 independent parts, one for each index of `run`. The reference program is written for one: setup_inputs(seed, part) draws one part's arguments, and reference() takes and returns one part's arrays. A program takes and returns all parts, laid end to end along the dimension named above; each array names one. Nothing has to cross between parts.
Inputs may be any that keep to these rules, and one draw needn't show every extreme that they name: ancestors come from systematic resampling with uneven weights, slots shuffled: some particles fill several slots, others none; particles 0 and 3 always fill some slot.
All inputs are finite; a program needn't handle non-finite values.
Results may differ from the reference program's by a relative error of at most 0.00055.
Values may be sent and summed in bfloat16 or wider, within the bound.
No kernel may reach another device: no remote copies, remote signals or barrier semaphores. Data moves between devices by JAX's collectives and lax.ppermute only.
A program may use at most 64 MiB of HBM per device.

```python
import jax
import jax.numpy as jnp

COLS = 1024
LEVELS = 2
FIELDS = 8
PARTICLES = 4
ROWS = 64


def draw_ancestors(key, part):
    key = jax.random.fold_in(key, 11)
    key_weight, key_offset, key_shuffle = jax.random.split(key, 3)
    heights = jax.random.randint(key_weight, (PARTICLES,), 1, 17)
    weights = heights * heights
    running_weight_sum = jnp.cumsum(weights)
    total_weight = running_weight_sum[-1]
    uniform_shift = jax.random.randint(key_offset, (), 0, total_weight)
    positions = (jnp.arange(PARTICLES, dtype=jnp.int32) * total_weight + uniform_shift) // PARTICLES
    picked_particle = jnp.sum((running_weight_sum[None, :] <= positions[:, None]).astype(jnp.int32), axis=1)
    shuffle = jax.random.permutation(key_shuffle, PARTICLES)
    picked_particle = picked_particle[shuffle]
    slot_index_list = jnp.arange(PARTICLES, dtype=jnp.int32)
    picked_particle = jnp.where(slot_index_list == shuffle[0], 0, picked_particle)
    picked_particle = jnp.where(slot_index_list == shuffle[1], PARTICLES - 1, picked_particle)
    return picked_particle.astype(jnp.int32)


def level_of(rng, dims, pieces, smallest, top_value):
    def one(dim, shards_of):
        draws = jax.random.uniform(jax.random.fold_in(jax.random.fold_in(rng, 6), dim), (shards_of,), jnp.float32, smallest / len(pieces), top_value / len(pieces))
        return jnp.repeat(jnp.exp(draws), dims[dim] // shards_of).reshape((-1,) + (1,) * (len(dims) - dim - 1))

    factor_of = one(*pieces[0])
    for cut in pieces[1:]:
        factor_of = factor_of * one(*cut)
    return factor_of


def scatter_about(rng, dims, scale, reach, shards=(), held_as=jnp.bfloat16):
    drawn = jax.random.normal(rng, dims, jnp.float32) * scale
    if len(shards) > 0:
        drawn = level_of(rng, dims, shards, -0.22, 0.18) * drawn
    return jnp.clip(drawn, min=-reach, max=reach).astype(held_as)


def setup_inputs(seed: int = 0, part: int = 0) -> dict:
    arg_keys = jax.random.split(jax.random.key(seed), 4)
    part_splits = jax.random.split(jax.random.fold_in(arg_keys[3], part), 4)
    return {
        "state": scatter_about(part_splits[0], (PARTICLES, FIELDS, ROWS, COLS), 1.0, 6.0, ((0, 4), (2, 4)), jnp.float32),
        "ancestors": draw_ancestors(jax.random.fold_in(jax.random.fold_in(arg_keys[3], part), 71), part),
        "noise": scatter_about(part_splits[2], (PARTICLES, LEVELS, ROWS, COLS), 1.0, 6.0, ((0, 4), (2, 4))),
    }


def pad_rows(field):
    widths = [(0, 0)] * (field.ndim - 2) + [(1, 1), (0, 0)]
    return jnp.pad(field, widths)


def split_levels(array):
    return array.reshape(array.shape[:-3] + (2, 4) + array.shape[-2:])


def advance(padded):
    middle = padded[..., 1:-1, :]
    north = padded[..., 2:, :]
    south = padded[..., :-2, :]
    east = jnp.roll(middle, -1, axis=-1)
    west = jnp.roll(middle, 1, axis=-1)
    fields = split_levels(middle)
    grad_x = split_levels(0.5 * (east - west))
    grad_y = split_levels(0.5 * (north - south))
    laplace = split_levels(east + west + north + south - 4.0 * middle)
    speed_u = fields[..., 0, :, :]
    speed_v = fields[..., 1, :, :]
    height = fields[..., 2, :, :]
    passive_scalar = fields[..., 3, :, :]
    hx = grad_x[..., 2, :, :]
    hy = grad_y[..., 2, :, :]
    press_x = jnp.stack([hx[..., 0, :, :] + hx[..., 1, :, :], hx[..., 0, :, :] + 1.6 * hx[..., 1, :, :]], axis=-3)
    press_y = jnp.stack([hy[..., 0, :, :] + hy[..., 1, :, :], hy[..., 0, :, :] + 1.6 * hy[..., 1, :, :]], axis=-3)
    depth = jnp.array([0.8, 0.5], dtype=jnp.float32).reshape(2, 1, 1)
    new_u = speed_u + 0.3 * speed_v - 0.25 * press_x - 0.05 * speed_u + 0.1 * laplace[..., 0, :, :]
    new_v = speed_v - 0.3 * speed_u - 0.25 * press_y - 0.05 * speed_v + 0.1 * laplace[..., 1, :, :]
    new_h = height - depth * (grad_x[..., 0, :, :] + grad_y[..., 1, :, :]) + 0.1 * laplace[..., 2, :, :]
    new_q = passive_scalar - 0.25 * (speed_u * grad_x[..., 3, :, :] + speed_v * grad_y[..., 3, :, :]) + 0.1 * laplace[..., 3, :, :]
    result = jnp.stack([new_u, new_v, new_h, new_q], axis=-3)
    return result.reshape(middle.shape)


def smooth(padded):
    middle = padded[..., 1:-1, :]
    total = 4.0 * middle + padded[..., 2:, :] + padded[..., :-2, :]
    total = total + jnp.roll(middle, -1, axis=-1) + jnp.roll(middle, 1, axis=-1)
    return 0.06 * total


def add_noise(resampled, smoothed):
    levels = split_levels(resampled)
    height = levels[:, :, 2:3] + smoothed[:, :, None]
    joined = jnp.concatenate([levels[:, :, :2], height, levels[:, :, 3:]], axis=2)
    return joined.reshape(resampled.shape)


def reference(state, ancestors, noise):
    current = state
    for substep in range(2):
        current = advance(pad_rows(current))
    resampled = jnp.take(current, ancestors, axis=0)
    smoothed = smooth(pad_rows(noise.astype(jnp.float32)))
    return add_noise(resampled, smoothed)
```

```python
import functools

import jax
import jax.numpy as jnp
from jax import lax
from jax.experimental import pallas as pl
from jax.experimental.pallas import tpu as pltpu
from jax.sharding import PartitionSpec as P

SCALE = 8192.0
WIRE = jnp.float16
DEPTHS = (0.8, 0.5)
SECOND = (1.0, 1.6)


def pack(values):
    return (values.astype(jnp.float32) * SCALE).astype(WIRE)


def unpack(values):
    return values.astype(jnp.float32) * (1.0 / SCALE)


def lane_roll(a, shift):
    return pltpu.roll(a, shift % a.shape[-1], a.ndim - 1)


def row_roll(a, shift):
    return pltpu.roll(a, shift % a.shape[-2], a.ndim - 2)


def neighbours(a, below=None, above=None):
    east, west = lane_roll(a, -1), lane_roll(a, 1)
    north, south = row_roll(a, -1), row_roll(a, 1)
    if below is not None:
        rows = a.shape[0]
        index = lax.broadcasted_iota(jnp.int32, a.shape, 0)
        north = jnp.where(index == rows - 1, above, north)
        south = jnp.where(index == 0, below, south)
    return east, west, north, south


def advance(fields, below=None, above=None):
    around = [
        neighbours(f, *((below[i], above[i]) if below is not None else ()))
        for i, f in enumerate(fields)
    ]
    out = []
    hx = [around[l * 4 + 2][0] - around[l * 4 + 2][1] for l in range(2)]
    hy = [around[l * 4 + 2][2] - around[l * 4 + 2][3] for l in range(2)]
    for l in range(2):
        u, v, h, q = fields[l * 4 : l * 4 + 4]
        eu, wu, nu, su = around[l * 4]
        ev, wv, nv, sv = around[l * 4 + 1]
        eh, wh, nh, sh = around[l * 4 + 2]
        eq, wq, nq, sq = around[l * 4 + 3]
        px = hx[0] + SECOND[l] * hx[1]
        py = hy[0] + SECOND[l] * hy[1]
        out.append(0.55 * u + 0.3 * v - 0.125 * px + 0.1 * (eu + wu + nu + su))
        out.append(0.55 * v - 0.3 * u - 0.125 * py + 0.1 * (ev + wv + nv + sv))
        out.append(
            0.6 * h
            - (0.5 * DEPTHS[l]) * ((eu - wu) + (nv - sv))
            + 0.1 * (eh + wh + nh + sh)
        )
        out.append(
            0.6 * q
            - 0.125 * (u * (eq - wq) + v * (nq - sq))
            + 0.1 * (eq + wq + nq + sq)
        )
    return out


def finish_kernel(parts, place_ref, *refs):
    piece_refs, (pair_ref, other_ref, noise_ref, out_ref, held, edge) = (
        refs[:parts],
        refs[parts:],
    )
    me = place_ref[0]
    even = place_ref[1] == 0
    width = held.shape[0] // parts
    fields_total, rows, cols = held.shape
    for m in range(parts):
        spot = pl.ds((me ^ m) * width, width)
        held[spot] = piece_refs[m][...]
        old = pl.ds(m * width, width)
        edge[0, spot] = jnp.where(even, other_ref[old], pair_ref[old])
        edge[1, spot] = jnp.where(even, pair_ref[old], other_ref[old])
    scale = 1.0 / SCALE
    fields = [held[f] for f in range(fields_total)]
    lower = [edge[0, f] * scale for f in range(fields_total)]
    upper = [edge[1, f] * scale for f in range(fields_total)]
    strip = [
        jnp.concatenate(
            [lower[f], fields[f][:1], fields[f][rows - 1 :], upper[f], upper[f]], axis=0
        )
        for f in range(fields_total)
    ]
    strip = advance(strip)
    first = advance(
        fields, [e[1:2] for e in lower], [e[0:1] for e in upper]
    )
    keep_low = jnp.where(place_ref[2] == 1, 0.0, 1.0)
    keep_high = jnp.where(place_ref[3] == 1, 0.0, 1.0)
    second = advance(
        first, [s[1:2] * keep_low for s in strip], [s[4:5] * keep_high for s in strip]
    )
    for f in range(fields_total):
        if f % 4 != 2:
            out_ref[f] = second[f]
    pair_noise = pair_ref[fields_total] * scale
    other_noise = other_ref[fields_total] * scale
    below = jnp.where(even, other_noise, pair_noise)
    above = jnp.where(even, pair_noise, other_noise)
    for l in range(2):
        n = noise_ref[l].astype(jnp.float32)
        e, w, no, so = neighbours(n, below[l : l + 1], above[l : l + 1])
        out_ref[l * 4 + 2] = second[l * 4 + 2] + 0.06 * (4.0 * n + e + w + no + so)


def finish(place, pieces, pair, other, noise):
    parts = len(pieces)
    fields = parts * pieces[0].shape[0]
    rows, cols = pieces[0].shape[1:]
    vmem = pl.BlockSpec(memory_space=pltpu.VMEM)
    return pl.pallas_call(
        functools.partial(finish_kernel, parts),
        out_shape=jax.ShapeDtypeStruct((fields, rows, cols), jnp.float32),
        in_specs=[pl.BlockSpec(memory_space=pltpu.SMEM)] + [vmem] * (parts + 3),
        out_specs=vmem,
        scratch_shapes=[
            pltpu.VMEM((fields, rows, cols), jnp.float32),
            pltpu.VMEM((2, fields, 2, cols), jnp.float32),
        ],
        compiler_params=pltpu.CompilerParams(vmem_limit_bytes=32 * 1024 * 1024),
        cost_estimate=pl.CostEstimate(
            flops=130 * fields * rows * cols, bytes_accessed=1 << 20, transcendentals=0
        ),
    )(place, *pieces, pair, other, noise)


def fetch_by_permutes(state, ancestors, count, me):
    def swap(a, m):
        return lax.ppermute(a, "particle", [(i, i ^ m) for i in range(count)])

    fields, rows, cols = state.shape
    cut = state.reshape(count, fields // count, rows, cols)

    def part(m):
        return pack(lax.dynamic_index_in_dim(cut, me ^ m, 0, keepdims=False))

    here = [part(0)] + [swap(part(m), m) for m in range(1, count)]

    def pick(slot):
        which = lax.dynamic_index_in_dim(ancestors, slot, 0, keepdims=False) ^ me
        chosen = here[0]
        for m in range(1, count):
            chosen = jnp.where(which == m, here[m], chosen)
        return chosen

    return [pick(me)] + [swap(pick(me ^ m), m) for m in range(1, count)]


def fetch_by_all_to_all(state, ancestors, count):
    fields, rows, cols = state.shape
    cut = pack(state).reshape(fields, rows, count, cols // count).transpose(2, 0, 1, 3)
    here = lax.all_to_all(cut, "particle", split_axis=0, concat_axis=0, tiled=True)
    chosen = jnp.take(here, ancestors, axis=0)
    back = lax.all_to_all(chosen, "particle", split_axis=0, concat_axis=0, tiled=True)
    return back.transpose(1, 2, 0, 3).reshape(fields, rows, cols)


def per_device(state, ancestors, noise):
    state, noise = state[0], noise[0]
    count = lax.axis_size("particle")
    me = lax.axis_index("particle")
    if count in (2, 4, 8):
        order = me
        pieces = fetch_by_permutes(state, ancestors, count, me)
    else:
        order = jnp.int32(0)
        pieces = [fetch_by_all_to_all(state, ancestors, count)]

    blocks = lax.axis_size("space")
    where = lax.axis_index("space")
    even = where % 2 == 0
    low = jnp.concatenate(
        [p[:, :2] for p in pieces] + [pack(noise[:, :1]).reshape(1, 2, -1)], axis=0
    )
    high = jnp.concatenate(
        [p[:, -2:] for p in pieces] + [pack(noise[:, -1:]).reshape(1, 2, -1)], axis=0
    )
    pairs = [(i, i ^ 1) for i in range(blocks)]
    others = [
        p for i in range(1, blocks - 1, 2) for p in ((i, i + 1), (i + 1, i))
    ]
    pair = lax.ppermute(jnp.where(even, high, low), "space", pairs)
    other = lax.ppermute(jnp.where(even, low, high), "space", others)

    place = jnp.stack(
        [order, where % 2, (where == 0).astype(jnp.int32), (where == blocks - 1).astype(jnp.int32)]
    ).astype(jnp.int32)
    out = finish(
        place,
        [unpack(p) for p in pieces],
        pair.astype(jnp.float32),
        other.astype(jnp.float32),
        noise,
    )
    return out[None]


def solution(mesh):
    in_specs = (
        P(("run", "particle"), None, "space", None),
        P("run"),
        P(("run", "particle"), None, "space", None),
    )
    out_specs = P(("run", "particle"), None, "space", None)
    return jax.shard_map(
        per_device, mesh=mesh, in_specs=in_specs, out_specs=out_specs, check_vma=False
    )
```

```python
import functools

import jax
import jax.numpy as jnp
from jax import lax
from jax.experimental import pallas as pl
from jax.experimental.pallas import tpu as pltpu
from jax.sharding import PartitionSpec as P

SCALE = 8192.0
WIRE = jnp.float16
DEPTHS = (0.8, 0.5)
SECOND = (1.0, 1.6)


def pack(values):
    return (values.astype(jnp.float32) * SCALE).astype(WIRE)


def unpack(values):
    return values.astype(jnp.float32) * (1.0 / SCALE)


def lane_roll(a, shift):
    return pltpu.roll(a, shift % a.shape[-1], a.ndim - 1)


def row_roll(a, shift):
    return pltpu.roll(a, shift % a.shape[-2], a.ndim - 2)


def advance(fields):
    around = [
        (lane_roll(f, -1), lane_roll(f, 1), row_roll(f, -1), row_roll(f, 1))
        for f in fields
    ]
    out = []
    hx = [around[l * 4 + 2][0] - around[l * 4 + 2][1] for l in range(2)]
    hy = [around[l * 4 + 2][2] - around[l * 4 + 2][3] for l in range(2)]
    for l in range(2):
        u, v, h, q = fields[l * 4 : l * 4 + 4]
        eu, wu, nu, su = around[l * 4]
        ev, wv, nv, sv = around[l * 4 + 1]
        eh, wh, nh, sh = around[l * 4 + 2]
        eq, wq, nq, sq = around[l * 4 + 3]
        px = hx[0] + SECOND[l] * hx[1]
        py = hy[0] + SECOND[l] * hy[1]
        out.append(0.55 * u + 0.3 * v - 0.125 * px + 0.1 * (eu + wu + nu + su))
        out.append(0.55 * v - 0.3 * u - 0.125 * py + 0.1 * (ev + wv + nv + sv))
        out.append(
            0.6 * h
            - (0.5 * DEPTHS[l]) * ((eu - wu) + (nv - sv))
            + 0.1 * (eh + wh + nh + sh)
        )
        out.append(
            0.6 * q
            - 0.125 * (u * (eq - wq) + v * (nq - sq))
            + 0.1 * (eq + wq + nq + sq)
        )
    return out


def smooth(n):
    around = lane_roll(n, -1) + lane_roll(n, 1) + row_roll(n, -1) + row_roll(n, 1)
    return 0.06 * (4.0 * n + around)


def inner_kernel(parts, *refs):
    piece_refs, (noise_ref, out_ref, raw_ref, once_ref, fog_ref, held) = (
        refs[:parts],
        refs[parts:],
    )
    me = lax.axis_index("particle") if parts > 1 else 0
    total, rows, cols = held.shape
    width = total // parts
    for m in range(parts):
        held[pl.ds((me ^ m) * width, width)] = piece_refs[m][...]
    fields = [held[f] for f in range(total)]
    first = advance(fields)
    for f in range(total):
        raw_ref[f, 2:4] = fields[f][:2]
        raw_ref[f, 4:6] = fields[f][rows - 2 :]
        once_ref[f, 2:4] = first[f][1:3]
        once_ref[f, 4:6] = first[f][rows - 3 : rows - 1]
    second = advance(first)
    for f in range(total):
        if f % 4 == 2:
            n = noise_ref[f // 4].astype(jnp.float32)
            fog_ref[f // 4, 1:4] = n[:3]
            fog_ref[f // 4, 4:7] = n[rows - 3 :]
            out_ref[f] = second[f] + smooth(n)
        else:
            out_ref[f] = second[f]


def ends_kernel(
    parts, inner_ref, raw_ref, once_ref, fog_ref, pair_ref, other_ref, out_hbm, out, sems
):
    me = lax.axis_index("particle") if parts > 1 else 0
    where = lax.axis_index("space")
    even = lax.rem(where, 2) == 0
    no_below, no_above = where == 0, where == lax.axis_size("space") - 1
    total, rows, cols = inner_ref.shape
    width = total // parts
    scale = 1.0 / SCALE

    def received(index):
        pair, other = pair_ref[index] * scale, other_ref[index] * scale
        return (
            jnp.where(no_below, 0.0, jnp.where(even, other, pair)),
            jnp.where(no_above, 0.0, jnp.where(even, pair, other)),
        )

    index = lax.broadcasted_iota(jnp.int32, (8, cols), 0)
    raw = []
    for f in range(total):
        below, above = received(((f // width) ^ me) * width + f % width)
        raw.append(jnp.concatenate([below, raw_ref[f, 2:6], above], axis=0))
    moved = advance(raw)
    once = [
        jnp.where(
            index < 2,
            row_roll(moved[f], -1),
            jnp.where(index > 5, row_roll(moved[f], 1), once_ref[f]),
        )
        for f in range(total)
    ]
    outside = (no_below & (index == 0)) | (no_above & (index == 7))
    once = [jnp.where(outside, 0.0, o) for o in once]
    twice = advance(once)
    fog_below, fog_above = received(total)
    sends = []
    for f in range(total):
        ends = twice[f]
        if f % 4 == 2:
            l = f // 4
            fog = jnp.concatenate(
                [fog_below[l : l + 1], fog_ref[l, 1:7], fog_above[l : l + 1]], axis=0
            )
            ends = ends + smooth(fog)
        out[f, :8] = jnp.where(index < 2, row_roll(ends, -1), inner_ref[f, :8])
        if rows > 16:
            out[f, 8 : rows - 8] = inner_ref[f, 8 : rows - 8]
        out[f, rows - 8 :] = jnp.where(
            index > 5, row_roll(ends, 1), inner_ref[f, rows - 8 :]
        )
        send = pltpu.make_async_copy(out.at[f], out_hbm.at[f], sems.at[f])
        send.start()
        sends.append(send)
    for send in sends:
        send.wait()


VMEM = pl.BlockSpec(memory_space=pltpu.VMEM)
PARAMS = pltpu.CompilerParams(vmem_limit_bytes=32 * 1024 * 1024)


def inner(pieces, noise):
    parts = len(pieces)
    total = parts * pieces[0].shape[0]
    rows, cols = pieces[0].shape[1:]
    shapes = [(total, rows, cols), (total, 8, cols), (total, 8, cols), (2, 8, cols)]
    return pl.pallas_call(
        functools.partial(inner_kernel, parts),
        out_shape=[jax.ShapeDtypeStruct(shape, jnp.float32) for shape in shapes],
        in_specs=[VMEM] * (parts + 1),
        out_specs=[VMEM] * 4,
        scratch_shapes=[pltpu.VMEM(shapes[0], jnp.float32)],
        compiler_params=PARAMS,
        cost_estimate=pl.CostEstimate(
            flops=110 * total * rows * cols, bytes_accessed=1 << 20, transcendentals=0
        ),
    )(*pieces, noise)


def ends(parts, kept, pair, other):
    total, rows, cols = kept[0].shape
    return pl.pallas_call(
        functools.partial(ends_kernel, parts),
        out_shape=jax.ShapeDtypeStruct((total, rows, cols), jnp.float32),
        in_specs=[VMEM] * 6,
        out_specs=pl.BlockSpec(memory_space=pl.ANY),
        scratch_shapes=[
            pltpu.VMEM((total, rows, cols), jnp.float32),
            pltpu.SemaphoreType.DMA((total,)),
        ],
        compiler_params=PARAMS,
        cost_estimate=pl.CostEstimate(
            flops=110 * total * 8 * cols, bytes_accessed=1 << 20, transcendentals=0
        ),
    )(*kept, pair, other)


def fetch_by_permutes(state, ancestors, count, me):
    def swap(a, m):
        return lax.ppermute(a, "particle", [(i, i ^ m) for i in range(count)])

    fields, rows, cols = state.shape
    cut = state.reshape(count, fields // count, rows, cols)

    def part(m):
        return pack(lax.dynamic_index_in_dim(cut, me ^ m, 0, keepdims=False))

    own, *sent = lax.optimization_barrier([part(m) for m in range(count)])
    here = [own] + [swap(sent[m - 1], m) for m in range(1, count)]

    code = jnp.sum((ancestors ^ me) << (4 * jnp.arange(count, dtype=jnp.int32)))

    def pick(slot):
        which = (code >> (4 * slot)) & (count - 1)
        chosen = here[0]
        for m in range(1, count):
            chosen = jnp.where(which == m, here[m], chosen)
        return chosen

    own, *sent = lax.optimization_barrier([pick(me ^ m) for m in range(count)])
    return [own] + [swap(sent[m - 1], m) for m in range(1, count)]


def fetch_by_all_to_all(state, ancestors, count):
    fields, rows, cols = state.shape
    cut = pack(state).reshape(fields, rows, count, cols // count).transpose(2, 0, 1, 3)
    here = lax.all_to_all(cut, "particle", split_axis=0, concat_axis=0, tiled=True)
    chosen = jnp.take(here, ancestors, axis=0)
    back = lax.all_to_all(chosen, "particle", split_axis=0, concat_axis=0, tiled=True)
    return back.transpose(1, 2, 0, 3).reshape(fields, rows, cols)


def per_device(state, ancestors, noise):
    state, noise = state[0], noise[0]
    count = lax.axis_size("particle")
    me = lax.axis_index("particle")
    if count in (2, 4, 8):
        pieces = fetch_by_permutes(state, ancestors, count, me)
    else:
        pieces = [fetch_by_all_to_all(state, ancestors, count)]

    blocks = lax.axis_size("space")
    where = lax.axis_index("space")
    even = where % 2 == 0
    low = jnp.concatenate(
        [p[:, :2] for p in pieces] + [pack(noise[:, :1]).reshape(1, 2, -1)], axis=0
    )
    high = jnp.concatenate(
        [p[:, -2:] for p in pieces] + [pack(noise[:, -1:]).reshape(1, 2, -1)], axis=0
    )
    pairs = [(i, i ^ 1) for i in range(blocks)]
    others = [(i, (i + 1 if i % 2 else i - 1) % blocks) for i in range(blocks)]
    pair = lax.ppermute(jnp.where(even, high, low), "space", pairs)
    other = lax.ppermute(jnp.where(even, low, high), "space", others)

    kept = inner([unpack(p) for p in pieces], noise)
    out = ends(
        len(pieces), kept, pair.astype(jnp.float32), other.astype(jnp.float32)
    )
    return out[None]


def solution(mesh):
    in_specs = (
        P(("run", "particle"), None, "space", None),
        P("run"),
        P(("run", "particle"), None, "space", None),
    )
    out_specs = P(("run", "particle"), None, "space", None)
    return jax.shard_map(
        per_device, mesh=mesh, in_specs=in_specs, out_specs=out_specs, check_vma=False
    )
```

```python
import functools

import jax
import jax.numpy as jnp
import numpy as np
from jax import lax
from jax.experimental import pallas as pl
from jax.experimental.pallas import tpu as pltpu
from jax.sharding import PartitionSpec as P

SCALE = 8192.0
WIRE = jnp.float16
DEPTHS = (0.8, 0.5)
SECOND = (1.0, 1.6)


ACROSS = 3
CHUNKS = 2


def pack(values):
    return (values.astype(jnp.float32) * SCALE).astype(WIRE)


def unpack(values):
    return values.astype(jnp.float32) * (1.0 / SCALE)


def lane_roll(a, shift):
    return pltpu.roll(a, shift % a.shape[-1], a.ndim - 1)


def row_roll(a, shift):
    return pltpu.roll(a, shift % a.shape[-2], a.ndim - 2)


def advance(fields):
    around = [
        (lane_roll(f, -1), lane_roll(f, 1), row_roll(f, -1), row_roll(f, 1))
        for f in fields
    ]
    out = []
    hx = [around[l * 4 + 2][0] - around[l * 4 + 2][1] for l in range(2)]
    hy = [around[l * 4 + 2][2] - around[l * 4 + 2][3] for l in range(2)]
    for l in range(2):
        u, v, h, q = fields[l * 4 : l * 4 + 4]
        eu, wu, nu, su = around[l * 4]
        ev, wv, nv, sv = around[l * 4 + 1]
        eh, wh, nh, sh = around[l * 4 + 2]
        eq, wq, nq, sq = around[l * 4 + 3]
        px = hx[0] + SECOND[l] * hx[1]
        py = hy[0] + SECOND[l] * hy[1]
        out.append(0.55 * u + 0.3 * v - 0.125 * px + 0.1 * (eu + wu + nu + su))
        out.append(0.55 * v - 0.3 * u - 0.125 * py + 0.1 * (ev + wv + nv + sv))
        out.append(
            0.6 * h
            - (0.5 * DEPTHS[l]) * ((eu - wu) + (nv - sv))
            + 0.1 * (eh + wh + nh + sh)
        )
        out.append(
            0.6 * q
            - 0.125 * (u * (eq - wq) + v * (nq - sq))
            + 0.1 * (eq + wq + nq + sq)
        )
    return out


def smooth(n):
    around = lane_roll(n, -1) + lane_roll(n, 1) + row_roll(n, -1) + row_roll(n, 1)
    return 0.06 * (4.0 * n + around)


def inner_kernel(parts, *refs):
    piece_refs, (noise_ref, out_ref, raw_ref, once_ref, fog_ref) = (
        refs[:parts],
        refs[parts:],
    )
    total, rows, cols = out_ref.shape
    fields = [ref[i] for ref in piece_refs for i in range(ref.shape[0])]
    first = advance(fields)
    for f in range(total):
        raw_ref[f, 2:4] = fields[f][:2]
        raw_ref[f, 4:6] = fields[f][rows - 2 :]
        once_ref[f, 2:4] = first[f][1:3]
        once_ref[f, 4:6] = first[f][rows - 3 : rows - 1]
    second = advance(first)
    for f in range(total):
        if f % 4 == 2:
            n = noise_ref[f // 4].astype(jnp.float32)
            fog_ref[f // 4, 1:4] = n[:3]
            fog_ref[f // 4, 4:7] = n[rows - 3 :]
            out_ref[f] = second[f] + smooth(n)
        else:
            out_ref[f] = second[f]


def ends_kernel(
    inner_ref, raw_ref, once_ref, fog_ref, pair_ref, other_ref, out_hbm, out, sems
):
    where = lax.axis_index("space")
    even = lax.rem(where, 2) == 0
    no_below, no_above = where == 0, where == lax.axis_size("space") - 1
    total, rows, cols = inner_ref.shape
    scale = 1.0 / SCALE

    def received(index):
        pair, other = pair_ref[index] * scale, other_ref[index] * scale
        return (
            jnp.where(no_below, 0.0, jnp.where(even, other, pair)),
            jnp.where(no_above, 0.0, jnp.where(even, pair, other)),
        )

    index = lax.broadcasted_iota(jnp.int32, (8, cols), 0)
    raw = []
    for f in range(total):
        below, above = received(f)
        raw.append(jnp.concatenate([below, raw_ref[f, 2:6], above], axis=0))
    moved = advance(raw)
    once = [
        jnp.where(
            index < 2,
            row_roll(moved[f], -1),
            jnp.where(index > 5, row_roll(moved[f], 1), once_ref[f]),
        )
        for f in range(total)
    ]
    outside = (no_below & (index == 0)) | (no_above & (index == 7))
    once = [jnp.where(outside, 0.0, o) for o in once]
    twice = advance(once)
    fog_below, fog_above = received(total)
    sends = []
    for f in range(total):
        ends = twice[f]
        if f % 4 == 2:
            l = f // 4
            fog = jnp.concatenate(
                [fog_below[l : l + 1], fog_ref[l, 1:7], fog_above[l : l + 1]], axis=0
            )
            ends = ends + smooth(fog)
        out[f, :8] = jnp.where(index < 2, row_roll(ends, -1), inner_ref[f, :8])
        if rows > 16:
            out[f, 8 : rows - 8] = inner_ref[f, 8 : rows - 8]
        out[f, rows - 8 :] = jnp.where(
            index > 5, row_roll(ends, 1), inner_ref[f, rows - 8 :]
        )
        send = pltpu.make_async_copy(out.at[f], out_hbm.at[f], sems.at[f])
        send.start()
        sends.append(send)
    for send in sends:
        send.wait()


VMEM = pl.BlockSpec(memory_space=pltpu.VMEM)
PARAMS = pltpu.CompilerParams(vmem_limit_bytes=32 * 1024 * 1024)


def inner(pieces, noise):
    parts = len(pieces)
    total = sum(p.shape[0] for p in pieces)
    rows, cols = pieces[0].shape[1:]
    shapes = [(total, rows, cols), (total, 8, cols), (total, 8, cols), (2, 8, cols)]
    return pl.pallas_call(
        functools.partial(inner_kernel, parts),
        out_shape=[jax.ShapeDtypeStruct(shape, jnp.float32) for shape in shapes],
        in_specs=[VMEM] * (parts + 1),
        out_specs=[VMEM] * 4,
        compiler_params=PARAMS,
        cost_estimate=pl.CostEstimate(
            flops=110 * total * rows * cols, bytes_accessed=1 << 20, transcendentals=0
        ),
    )(*pieces, noise)


def ends(kept, pair, other):
    total, rows, cols = kept[0].shape
    return pl.pallas_call(
        ends_kernel,
        out_shape=jax.ShapeDtypeStruct((total, rows, cols), jnp.float32),
        in_specs=[VMEM] * 6,
        out_specs=pl.BlockSpec(memory_space=pl.ANY),
        scratch_shapes=[
            pltpu.VMEM((total, rows, cols), jnp.float32),
            pltpu.SemaphoreType.DMA((total,)),
        ],
        compiler_params=PARAMS,
        cost_estimate=pl.CostEstimate(
            flops=110 * total * 8 * cols, bytes_accessed=1 << 20, transcendentals=0
        ),
    )(*kept, pair, other)


def fetch_by_permutes(state, ancestors, me, even):
    blocks = lax.axis_size("space")

    def swap(a, even_mask, odd_mask):
        masks = (even_mask, odd_mask)
        pairs = [
            (i * blocks + s, (i ^ masks[s % 2]) * blocks + s)
            for i in range(4)
            for s in range(blocks)
        ]
        return lax.ppermute(a, ("particle", "space"), pairs)

    size = state.shape[0] // CHUNKS
    parts = [state[c * size : (c + 1) * size] for c in range(CHUNKS)]
    owns = lax.optimization_barrier([pack(p) for p in parts])
    gots = [swap(own, 1, ACROSS) for own in owns]
    places = 4 * np.arange(4, dtype=np.int32)
    code = jnp.sum(ancestors << places) ^ (me * np.sum(1 << places).astype(np.int32))
    first = jnp.where(even, 1, ACROSS)
    second = jnp.where(even, ACROSS, 1)

    def distance(slot):
        return (code >> (4 * slot)) & 3

    keep = distance(me ^ second) == 0
    mine = distance(me)
    result = []
    for own, got in zip(owns, gots):
        last = swap(jnp.where(keep, own, got), ACROSS, 1)
        result.append(jnp.where(mine == 0, own, jnp.where(mine == first, got, last)))
    return result


def fetch_by_all_to_all(state, ancestors, count):
    fields, rows, cols = state.shape
    cut = pack(state).reshape(fields, rows, count, cols // count).transpose(2, 0, 1, 3)
    here = lax.all_to_all(cut, "particle", split_axis=0, concat_axis=0, tiled=True)
    chosen = jnp.take(here, ancestors, axis=0)
    back = lax.all_to_all(chosen, "particle", split_axis=0, concat_axis=0, tiled=True)
    return back.transpose(1, 2, 0, 3).reshape(fields, rows, cols)


def per_device(state, ancestors, noise):
    state, noise = state[0], noise[0]
    count = lax.axis_size("particle")
    me = lax.axis_index("particle")
    blocks = lax.axis_size("space")
    even = lax.axis_index("space") & 1 == 0
    if count == 4:
        pieces = fetch_by_permutes(state, ancestors, me, even)
    else:
        pieces = [fetch_by_all_to_all(state, ancestors, count)]

    fog_low = pack(noise[:, :1]).reshape(1, 2, -1)
    fog_high = pack(noise[:, -1:]).reshape(1, 2, -1)
    sides = [(p[:, :2], p[:, -2:]) for p in pieces] + [(fog_low, fog_high)]
    to_pair = jnp.concatenate([jnp.where(even, h, l) for l, h in sides], axis=0)
    to_other = jnp.concatenate([jnp.where(even, l, h) for l, h in sides], axis=0)
    to_other, to_pair = lax.optimization_barrier((to_other, to_pair))
    pairs = [(i, i ^ 1) for i in range(blocks)]
    others = [(i, (i + 1 if i % 2 else i - 1) % blocks) for i in range(blocks)]
    other = lax.ppermute(to_other, "space", others)
    pair = lax.ppermute(to_pair, "space", pairs)

    kept = inner([unpack(p) for p in pieces], noise)
    out = ends(kept, pair.astype(jnp.float32), other.astype(jnp.float32))
    return out[None]


def solution(mesh):
    in_specs = (
        P(("run", "particle"), None, "space", None),
        P("run"),
        P(("run", "particle"), None, "space", None),
    )
    out_specs = P(("run", "particle"), None, "space", None)
    return jax.shard_map(
        per_device, mesh=mesh, in_specs=in_specs, out_specs=out_specs, check_vma=False
    )
```

```python
import functools

import jax
import jax.numpy as jnp
import numpy as np
from jax import lax
from jax.experimental import pallas as pl
from jax.experimental.pallas import tpu as pltpu
from jax.sharding import PartitionSpec as P

SCALE = 8192.0
WIRE = jnp.float16
DEPTHS = (0.8, 0.5)
SECOND = (1.0, 1.6)


PLAN = (
    ((1, 2), (2, 1)),
    ((1, 3), (2, 1)),
)


def pack(values):
    return (values.astype(jnp.float32) * SCALE).astype(WIRE)


def unpack(values):
    return values.astype(jnp.float32) * (1.0 / SCALE)


def lane_roll(a, shift):
    return pltpu.roll(a, shift % a.shape[-1], a.ndim - 1)


def row_roll(a, shift):
    return pltpu.roll(a, shift % a.shape[-2], a.ndim - 2)


def advance(fields):
    around = [
        (lane_roll(f, -1), lane_roll(f, 1), row_roll(f, -1), row_roll(f, 1))
        for f in fields
    ]
    out = []
    hx = [around[l * 4 + 2][0] - around[l * 4 + 2][1] for l in range(2)]
    hy = [around[l * 4 + 2][2] - around[l * 4 + 2][3] for l in range(2)]
    for l in range(2):
        u, v, h, q = fields[l * 4 : l * 4 + 4]
        eu, wu, nu, su = around[l * 4]
        ev, wv, nv, sv = around[l * 4 + 1]
        eh, wh, nh, sh = around[l * 4 + 2]
        eq, wq, nq, sq = around[l * 4 + 3]
        px = hx[0] + SECOND[l] * hx[1]
        py = hy[0] + SECOND[l] * hy[1]
        out.append(0.55 * u + 0.3 * v - 0.125 * px + 0.1 * (eu + wu + nu + su))
        out.append(0.55 * v - 0.3 * u - 0.125 * py + 0.1 * (ev + wv + nv + sv))
        out.append(
            0.6 * h
            - (0.5 * DEPTHS[l]) * ((eu - wu) + (nv - sv))
            + 0.1 * (eh + wh + nh + sh)
        )
        out.append(
            0.6 * q
            - 0.125 * (u * (eq - wq) + v * (nq - sq))
            + 0.1 * (eq + wq + nq + sq)
        )
    return out


def smooth(n):
    around = lane_roll(n, -1) + lane_roll(n, 1) + row_roll(n, -1) + row_roll(n, 1)
    return 0.06 * (4.0 * n + around)


def inner_kernel(parts, *refs):
    piece_refs, (noise_ref, out_ref, raw_ref, once_ref, fog_ref) = (
        refs[:parts],
        refs[parts:],
    )
    total, rows, cols = out_ref.shape
    fields = [ref[i] for ref in piece_refs for i in range(ref.shape[0])]
    first = advance(fields)
    for f in range(total):
        raw_ref[f, 2:4] = fields[f][:2]
        raw_ref[f, 4:6] = fields[f][rows - 2 :]
        once_ref[f, 2:4] = first[f][1:3]
        once_ref[f, 4:6] = first[f][rows - 3 : rows - 1]
    second = advance(first)
    for f in range(total):
        if f % 4 == 2:
            n = noise_ref[f // 4].astype(jnp.float32)
            fog_ref[f // 4, 1:4] = n[:3]
            fog_ref[f // 4, 4:7] = n[rows - 3 :]
            out_ref[f] = second[f] + smooth(n)
        else:
            out_ref[f] = second[f]


def ends_kernel(
    inner_ref, raw_ref, once_ref, fog_ref, pair_ref, other_ref, out_hbm, out, sems
):
    where = lax.axis_index("space")
    even = lax.rem(where, 2) == 0
    no_below, no_above = where == 0, where == lax.axis_size("space") - 1
    total, rows, cols = inner_ref.shape
    scale = 1.0 / SCALE

    def received(index):
        pair, other = pair_ref[index] * scale, other_ref[index] * scale
        return (
            jnp.where(no_below, 0.0, jnp.where(even, other, pair)),
            jnp.where(no_above, 0.0, jnp.where(even, pair, other)),
        )

    index = lax.broadcasted_iota(jnp.int32, (8, cols), 0)
    raw = []
    for f in range(total):
        below, above = received(f)
        raw.append(jnp.concatenate([below, raw_ref[f, 2:6], above], axis=0))
    moved = advance(raw)
    once = [
        jnp.where(
            index < 2,
            row_roll(moved[f], -1),
            jnp.where(index > 5, row_roll(moved[f], 1), once_ref[f]),
        )
        for f in range(total)
    ]
    outside = (no_below & (index == 0)) | (no_above & (index == 7))
    once = [jnp.where(outside, 0.0, o) for o in once]
    twice = advance(once)
    fog_below, fog_above = received(total)
    sends = []
    for f in range(total):
        ends = twice[f]
        if f % 4 == 2:
            l = f // 4
            fog = jnp.concatenate(
                [fog_below[l : l + 1], fog_ref[l, 1:7], fog_above[l : l + 1]], axis=0
            )
            ends = ends + smooth(fog)
        out[f, :8] = jnp.where(index < 2, row_roll(ends, -1), inner_ref[f, :8])
        if rows > 16:
            out[f, 8 : rows - 8] = inner_ref[f, 8 : rows - 8]
        out[f, rows - 8 :] = jnp.where(
            index > 5, row_roll(ends, 1), inner_ref[f, rows - 8 :]
        )
        send = pltpu.make_async_copy(out.at[f], out_hbm.at[f], sems.at[f])
        send.start()
        sends.append(send)
    for send in sends:
        send.wait()


VMEM = pl.BlockSpec(memory_space=pltpu.VMEM)
PARAMS = pltpu.CompilerParams(vmem_limit_bytes=32 * 1024 * 1024)


def inner(pieces, noise):
    parts = len(pieces)
    total = sum(p.shape[0] for p in pieces)
    rows, cols = pieces[0].shape[1:]
    shapes = [(total, rows, cols), (total, 8, cols), (total, 8, cols), (2, 8, cols)]
    return pl.pallas_call(
        functools.partial(inner_kernel, parts),
        out_shape=[jax.ShapeDtypeStruct(shape, jnp.float32) for shape in shapes],
        in_specs=[VMEM] * (parts + 1),
        out_specs=[VMEM] * 4,
        compiler_params=PARAMS,
        cost_estimate=pl.CostEstimate(
            flops=110 * total * rows * cols, bytes_accessed=1 << 20, transcendentals=0
        ),
    )(*pieces, noise)


def ends(kept, pair, other):
    total, rows, cols = kept[0].shape
    return pl.pallas_call(
        ends_kernel,
        out_shape=jax.ShapeDtypeStruct((total, rows, cols), jnp.float32),
        in_specs=[VMEM] * 6,
        out_specs=pl.BlockSpec(memory_space=pl.ANY),
        scratch_shapes=[
            pltpu.VMEM((total, rows, cols), jnp.float32),
            pltpu.SemaphoreType.DMA((total,)),
        ],
        compiler_params=PARAMS,
        cost_estimate=pl.CostEstimate(
            flops=110 * total * 8 * cols, bytes_accessed=1 << 20, transcendentals=0
        ),
    )(*kept, pair, other)


def fetch_by_permutes(state, ancestors, me, even):
    blocks = lax.axis_size("space")

    def swap(a, masks):
        pairs = [
            (i * blocks + s, (i ^ masks[s % 2]) * blocks + s)
            for i in range(4)
            for s in range(blocks)
        ]
        return lax.ppermute(a, ("particle", "space"), pairs)

    def by_block(masks):
        return jnp.where(even, *masks)

    size = state.shape[0] // len(PLAN)
    parts = [state[c * size : (c + 1) * size] for c in range(len(PLAN))]
    owns = lax.optimization_barrier([pack(p) for p in parts])
    gots = [swap(own, first) for own, (first, _) in zip(owns, PLAN)]
    places = 4 * np.arange(4, dtype=np.int32)
    code = jnp.sum(ancestors << places) ^ (me * np.sum(1 << places).astype(np.int32))

    def distance(slot):
        return (code >> (4 * slot)) & 3

    mine = distance(me)
    result = []
    for own, got, (first, second) in zip(owns, gots, PLAN):
        give = jnp.where(distance(me ^ by_block(second)) == 0, own, got)
        last = swap(give, second)
        result.append(
            jnp.where(mine == 0, own, jnp.where(mine == by_block(first), got, last))
        )
    return result


def fetch_by_all_to_all(state, ancestors, count):
    fields, rows, cols = state.shape
    cut = pack(state).reshape(fields, rows, count, cols // count).transpose(2, 0, 1, 3)
    here = lax.all_to_all(cut, "particle", split_axis=0, concat_axis=0, tiled=True)
    chosen = jnp.take(here, ancestors, axis=0)
    back = lax.all_to_all(chosen, "particle", split_axis=0, concat_axis=0, tiled=True)
    return back.transpose(1, 2, 0, 3).reshape(fields, rows, cols)


def per_device(state, ancestors, noise):
    state, noise = state[0], noise[0]
    count = lax.axis_size("particle")
    me = lax.axis_index("particle")
    blocks = lax.axis_size("space")
    even = lax.axis_index("space") & 1 == 0
    if count == 4:
        pieces = fetch_by_permutes(state, ancestors, me, even)
    else:
        pieces = [fetch_by_all_to_all(state, ancestors, count)]

    fog_low = pack(noise[:, :1]).reshape(1, 2, -1)
    fog_high = pack(noise[:, -1:]).reshape(1, 2, -1)
    sides = [(p[:, :2], p[:, -2:]) for p in pieces] + [(fog_low, fog_high)]
    to_pair = jnp.concatenate([jnp.where(even, h, l) for l, h in sides], axis=0)
    to_other = jnp.concatenate([jnp.where(even, l, h) for l, h in sides], axis=0)
    to_other, to_pair = lax.optimization_barrier((to_other, to_pair))
    pairs = [(i, i ^ 1) for i in range(blocks)]
    others = [(i, (i + 1 if i % 2 else i - 1) % blocks) for i in range(blocks)]
    other = lax.ppermute(to_other, "space", others)
    pair = lax.ppermute(to_pair, "space", pairs)

    kept = inner([unpack(p) for p in pieces], noise)
    out = ends(kept, pair.astype(jnp.float32), other.astype(jnp.float32))
    return out[None]


def solution(mesh):
    in_specs = (
        P(("run", "particle"), None, "space", None),
        P("run"),
        P(("run", "particle"), None, "space", None),
    )
    out_specs = P(("run", "particle"), None, "space", None)
    return jax.shard_map(
        per_device, mesh=mesh, in_specs=in_specs, out_specs=out_specs, check_vma=False
    )
```

```python
import functools

import jax
import jax.numpy as jnp
import numpy as np
from jax import lax
from jax.experimental import pallas as pl
from jax.experimental.pallas import tpu as pltpu
from jax.sharding import PartitionSpec as P

SCALE = 8192.0
WIRE = jnp.float16
DEPTHS = (0.8, 0.5)
SECOND = (1.0, 1.6)


PLAN = (
    ((1, 2), (2, 1)),
    ((1, 3), (2, 1)),
)


def pack(values):
    return (values.astype(jnp.float32) * SCALE).astype(WIRE)


def unpack(values):
    return values.astype(jnp.float32) * (1.0 / SCALE)


def lane_roll(a, shift):
    return pltpu.roll(a, shift % a.shape[-1], a.ndim - 1)


def row_roll(a, shift):
    return pltpu.roll(a, shift % a.shape[-2], a.ndim - 2)


def advance(fields):
    around = [
        (lane_roll(f, -1), lane_roll(f, 1), row_roll(f, -1), row_roll(f, 1))
        for f in fields
    ]
    out = []
    hx = [around[l * 4 + 2][0] - around[l * 4 + 2][1] for l in range(2)]
    hy = [around[l * 4 + 2][2] - around[l * 4 + 2][3] for l in range(2)]
    for l in range(2):
        u, v, h, q = fields[l * 4 : l * 4 + 4]
        eu, wu, nu, su = around[l * 4]
        ev, wv, nv, sv = around[l * 4 + 1]
        eh, wh, nh, sh = around[l * 4 + 2]
        eq, wq, nq, sq = around[l * 4 + 3]
        px = hx[0] + SECOND[l] * hx[1]
        py = hy[0] + SECOND[l] * hy[1]
        out.append(0.55 * u + 0.3 * v - 0.125 * px + 0.1 * (eu + wu + nu + su))
        out.append(0.55 * v - 0.3 * u - 0.125 * py + 0.1 * (ev + wv + nv + sv))
        out.append(
            0.6 * h
            - (0.5 * DEPTHS[l]) * ((eu - wu) + (nv - sv))
            + 0.1 * (eh + wh + nh + sh)
        )
        out.append(
            0.6 * q
            - 0.125 * (u * (eq - wq) + v * (nq - sq))
            + 0.1 * (eq + wq + nq + sq)
        )
    return out


def smooth(n):
    around = lane_roll(n, -1) + lane_roll(n, 1) + row_roll(n, -1) + row_roll(n, 1)
    return 0.06 * (4.0 * n + around)


def inner_kernel(parts, *refs):
    piece_refs, (noise_ref, out_ref, raw_ref, once_ref, fog_ref) = (
        refs[:parts],
        refs[parts:],
    )
    total, rows, cols = out_ref.shape
    fields = [ref[i] for ref in piece_refs for i in range(ref.shape[0])]
    first = advance(fields)
    for f in range(total):
        raw_ref[f, 2:4] = fields[f][:2]
        raw_ref[f, 4:6] = fields[f][rows - 2 :]
        once_ref[f, 2:4] = first[f][1:3]
        once_ref[f, 4:6] = first[f][rows - 3 : rows - 1]
    second = advance(first)
    for f in range(total):
        if f % 4 == 2:
            n = noise_ref[f // 4].astype(jnp.float32)
            fog_ref[f // 4, 1:4] = n[:3]
            fog_ref[f // 4, 4:7] = n[rows - 3 :]
            out_ref[f] = second[f] + smooth(n)
        else:
            out_ref[f] = second[f]


def ends_kernel(
    inner_ref, raw_ref, once_ref, fog_ref, other_ref, pair_ref, out_hbm, out, sems
):
    where = lax.axis_index("space")
    even = lax.rem(where, 2) == 0
    no_below, no_above = where == 0, where == lax.axis_size("space") - 1
    total, rows, cols = inner_ref.shape
    scale = 1.0 / SCALE

    def received(index):
        pair, other = pair_ref[index] * scale, other_ref[index] * scale
        return (
            jnp.where(no_below, 0.0, jnp.where(even, other, pair)),
            jnp.where(no_above, 0.0, jnp.where(even, pair, other)),
        )

    index = lax.broadcasted_iota(jnp.int32, (8, cols), 0)
    raw = []
    for f in range(total):
        below, above = received(f)
        raw.append(jnp.concatenate([below, raw_ref[f, 2:6], above], axis=0))
    moved = advance(raw)
    once = [
        jnp.where(
            index < 2,
            row_roll(moved[f], -1),
            jnp.where(index > 5, row_roll(moved[f], 1), once_ref[f]),
        )
        for f in range(total)
    ]
    outside = (no_below & (index == 0)) | (no_above & (index == 7))
    once = [jnp.where(outside, 0.0, o) for o in once]
    twice = advance(once)
    fog_below, fog_above = received(total)
    sends = []
    for f in range(total):
        ends = twice[f]
        if f % 4 == 2:
            l = f // 4
            fog = jnp.concatenate(
                [fog_below[l : l + 1], fog_ref[l, 1:7], fog_above[l : l + 1]], axis=0
            )
            ends = ends + smooth(fog)
        out[f, :8] = jnp.where(index < 2, row_roll(ends, -1), inner_ref[f, :8])
        if rows > 16:
            out[f, 8 : rows - 8] = inner_ref[f, 8 : rows - 8]
        out[f, rows - 8 :] = jnp.where(
            index > 5, row_roll(ends, 1), inner_ref[f, rows - 8 :]
        )
        send = pltpu.make_async_copy(out.at[f], out_hbm.at[f], sems.at[f])
        send.start()
        sends.append(send)
    for send in sends:
        send.wait()


VMEM = pl.BlockSpec(memory_space=pltpu.VMEM)
PARAMS = pltpu.CompilerParams(vmem_limit_bytes=32 * 1024 * 1024)


def inner(pieces, noise):
    parts = len(pieces)
    total = sum(p.shape[0] for p in pieces)
    rows, cols = pieces[0].shape[1:]
    shapes = [(total, rows, cols), (total, 8, cols), (total, 8, cols), (2, 8, cols)]
    return pl.pallas_call(
        functools.partial(inner_kernel, parts),
        out_shape=[jax.ShapeDtypeStruct(shape, jnp.float32) for shape in shapes],
        in_specs=[VMEM] * (parts + 1),
        out_specs=[VMEM] * 4,
        compiler_params=PARAMS,
        cost_estimate=pl.CostEstimate(
            flops=110 * total * rows * cols, bytes_accessed=1 << 20, transcendentals=0
        ),
    )(*pieces, noise)


def ends(kept, other, pair):
    total, rows, cols = kept[0].shape
    return pl.pallas_call(
        ends_kernel,
        out_shape=jax.ShapeDtypeStruct((total, rows, cols), jnp.float32),
        in_specs=[VMEM] * 6,
        out_specs=pl.BlockSpec(memory_space=pl.ANY),
        scratch_shapes=[
            pltpu.VMEM((total, rows, cols), jnp.float32),
            pltpu.SemaphoreType.DMA((total,)),
        ],
        compiler_params=PARAMS,
        cost_estimate=pl.CostEstimate(
            flops=110 * total * 8 * cols, bytes_accessed=1 << 20, transcendentals=0
        ),
    )(*kept, other, pair)


def fetch_by_permutes(state, ancestors, me, even):
    blocks = lax.axis_size("space")

    def swap(a, masks):
        pairs = [
            (i * blocks + s, (i ^ masks[s % 2]) * blocks + s)
            for i in range(4)
            for s in range(blocks)
        ]
        return lax.ppermute(a, ("particle", "space"), pairs)

    def by_block(masks):
        return jnp.where(even, *masks)

    size = state.shape[0] // len(PLAN)
    parts = [state[c * size : (c + 1) * size] for c in range(len(PLAN))]
    later = lax.optimization_barrier(state)[size:]
    owns = [lax.optimization_barrier(pack(p)) for p in (parts[0], later)]
    gots = [swap(own, first) for own, (first, _) in zip(owns, PLAN)]
    places = 4 * np.arange(4, dtype=np.int32)
    code = jnp.sum(ancestors << places) ^ (me * np.sum(1 << places).astype(np.int32))

    def distance(slot):
        return (code >> (4 * slot)) & 3

    mine = distance(me)
    result = []
    for own, got, (first, second) in zip(owns, gots, PLAN):
        give = jnp.where(distance(me ^ by_block(second)) == 0, own, got)
        last = swap(give, second)
        result.append(
            jnp.where(mine == 0, own, jnp.where(mine == by_block(first), got, last))
        )
    return result


def fetch_by_all_to_all(state, ancestors, count):
    fields, rows, cols = state.shape
    cut = pack(state).reshape(fields, rows, count, cols // count).transpose(2, 0, 1, 3)
    here = lax.all_to_all(cut, "particle", split_axis=0, concat_axis=0, tiled=True)
    chosen = jnp.take(here, ancestors, axis=0)
    back = lax.all_to_all(chosen, "particle", split_axis=0, concat_axis=0, tiled=True)
    return back.transpose(1, 2, 0, 3).reshape(fields, rows, cols)


def per_device(state, ancestors, noise):
    state, noise = state[0], noise[0]
    count = lax.axis_size("particle")
    me = lax.axis_index("particle")
    blocks = lax.axis_size("space")
    even = lax.axis_index("space") & 1 == 0
    if count == 4:
        pieces = fetch_by_permutes(state, ancestors, me, even)
    else:
        pieces = [fetch_by_all_to_all(state, ancestors, count)]

    fog_low = pack(noise[:, :1]).reshape(1, 2, -1)
    fog_high = pack(noise[:, -1:]).reshape(1, 2, -1)
    sides = [(p[:, :2], p[:, -2:]) for p in pieces] + [(fog_low, fog_high)]
    to_pair = jnp.concatenate([jnp.where(even, h, l) for l, h in sides], axis=0)
    to_other = jnp.concatenate([jnp.where(even, l, h) for l, h in sides], axis=0)
    to_other, to_pair, pieces = lax.optimization_barrier((to_other, to_pair, pieces))
    pairs = [(i, i ^ 1) for i in range(blocks)]
    others = [(i, (i + 1 if i % 2 else i - 1) % blocks) for i in range(blocks)]
    other = lax.ppermute(to_other, "space", others)
    pair = lax.ppermute(to_pair, "space", pairs)

    kept = inner([unpack(p) for p in pieces], noise)
    out = ends(kept, other.astype(jnp.float32), pair.astype(jnp.float32))
    return out[None]


def solution(mesh):
    in_specs = (
        P(("run", "particle"), None, "space", None),
        P("run"),
        P(("run", "particle"), None, "space", None),
    )
    out_specs = P(("run", "particle"), None, "space", None)
    return jax.shard_map(
        per_device, mesh=mesh, in_specs=in_specs, out_specs=out_specs, check_vma=False
    )
```
